32 devices in a mesh: row: 4 (over x, core), col: 8 (over z, y).
Axes of the slice: x: 2, y: 2, z: 4, core: 2. Of those that a mesh axis runs over, the one named last changes fastest.
Arguments:
- eta_pairs: bfloat16 [12288, 12288], P('row', 'col'), may hold values from -6 to 6
- gamma_pairs: bfloat16 [12288, 12288], P('row', 'col'), may hold values from -0.0546875 to 0.0546875
- pair_first: int32 [12288], P('row'), may hold values from 0 to 239
- pair_second: int32 [12288], P('row'), may hold values from 0 to 239
- occupancy: float32 [240], replicated, may hold values from 0 to 1
- gamma_recoupled: bfloat16 [32, 1536, 1536], P(('row', 'col')), may hold values from -0.15625 to 0.15625
- ph_factor: float32 [32, 1536], P(('row', 'col')), may hold values from -1 to 1
- tile_source: int32 [32, 576], P(('row', 'col')), may hold values from 0 to 287, as said below
- tile_owner: int32 [32, 576], P(('row', 'col')), may hold values from 0 to 31, as said below
- tile_place: int32 [32, 576], P(('row', 'col')), may hold values from 0 to 143
- sixj_weight: bfloat16 [32, 576], P(('row', 'col')), may hold values from -1 to 1
- live_count: int32 [32], P(('row', 'col')), may hold values from 288 to 576, as said below
Outputs:
- panel_update: bfloat16 [1024, 12288], P('col', 'row')
- recoupled_update: bfloat16 [12288, 12288], P('row', 'col')
The draws below stay inside these ranges and needn't reach their ends.
Inputs may be any that keep to these rules, and one draw needn't show every extreme that they name: `tile_source`: in each row the first 288 entries name every tile of the block once. `tile_owner`: in each row no channel is named by more than 18 entries; one channel is named exactly 18 times within the first 288 entries of every row. `live_count`: some block has 576 live slots and another 288.
All inputs are finite; a program needn't handle non-finite values.
Results may differ from the reference program's by a relative error of at most 0.019.
Values may be sent and summed in bfloat16 or wider, within the bound.
A program may use at most 192 MiB of HBM per device.

```python
import jax
import jax.numpy as jnp
from jax import lax

TILE = 128
PAIRS = 12288
ORBITS = 240
PH_STATES = 1536
PANEL_DEV = 128
BLOCK_ROWS = 3072
BLOCK_COLS = 1536
PANEL = 1024
BLOCKS = 32
TILES_BLOCK = 288
SLOTS = 576
CAP = 18
PH_TILES = 12
N_ROW = 4
N_COL = 8


def draw_tile_source(key, part):
    key = jax.random.fold_in(key, 11)
    cover_key, extra_key = jax.random.split(key)

    def one_row(row_key):
        return jax.random.permutation(row_key, TILES_BLOCK).astype(jnp.int32)
    covering = jax.vmap(one_row)(jax.random.split(cover_key, BLOCKS))
    extra = jax.random.randint(extra_key, (BLOCKS, SLOTS - TILES_BLOCK), 0, TILES_BLOCK).astype(jnp.int32)
    return jnp.concatenate([covering, extra], axis=1)


def draw_tile_owner(key, part):
    key = jax.random.fold_in(key, 23)
    busy_key, rows_key = jax.random.split(key)
    busiest = jax.random.randint(busy_key, (), 0, BLOCKS).astype(jnp.int32)
    spare_ids = jnp.arange((BLOCKS - 1) * CAP, dtype=jnp.int32) // CAP
    spare_ids = spare_ids + (spare_ids >= busiest).astype(jnp.int32)

    def one_row(row_key):
        sub_keys = jax.random.split(row_key, 3)
        shuffled = jax.random.permutation(sub_keys[0], spare_ids)[:SLOTS - CAP]
        row_owners = jnp.concatenate([jnp.full((CAP,), busiest, jnp.int32), shuffled])
        leading = jax.random.permutation(sub_keys[1], row_owners[:TILES_BLOCK])
        trailing = jax.random.permutation(sub_keys[2], row_owners[TILES_BLOCK:])
        return jnp.concatenate([leading, trailing]).astype(jnp.int32)
    return jax.vmap(one_row)(jax.random.split(rows_key, BLOCKS))


def draw_live_count(key, part):
    key = jax.random.fold_in(key, 37)
    sub_keys = jax.random.split(key, 3)
    counts = jax.random.randint(sub_keys[0], (BLOCKS,), TILES_BLOCK, SLOTS + 1).astype(jnp.int32)
    full_row = jax.random.randint(sub_keys[1], (), 0, BLOCKS)
    least_row = (full_row + 1 + jax.random.randint(sub_keys[2], (), 0, BLOCKS - 1)) % BLOCKS
    return counts.at[full_row].set(SLOTS).at[least_row].set(TILES_BLOCK).astype(jnp.int32)


def with_ends(result, rng, low, top_value):
    spot = [jax.random.randint(jax.random.fold_in(rng, axis), (), 0, length) for axis, length in enumerate(result.shape)]
    longest = result.shape.index(max(result.shape))
    neighbour = spot[:longest] + [(spot[longest] + 1) % result.shape[longest]] + spot[longest + 1:]
    return result.at[tuple(spot)].set(low).at[tuple(neighbour)].set(top_value)


def levels(stream_key, shape, cuts, smallest, high):
    def one(axis_at, blocks):
        heights = jax.random.uniform(jax.random.fold_in(jax.random.fold_in(stream_key, 6), axis_at), (blocks,), jnp.float32, smallest / len(cuts), high / len(cuts))
        return jnp.repeat(jnp.exp(heights), shape[axis_at] // blocks).reshape((-1,) + (1,) * (len(shape) - axis_at - 1))

    loudness = one(*cuts[0])
    for cut in cuts[1:]:
        loudness = loudness * one(*cut)
    return loudness


def noise(rng, dims, scale, most, pieces=(), held_as=jnp.bfloat16):
    level = levels(rng, dims, pieces, -0.22, 0.18) if pieces else 1.0
    result = jax.random.normal(rng, dims, jnp.float32) * scale * level
    return jnp.minimum(jnp.maximum(result, -most), most).astype(held_as)


def setup_inputs(seed: int = 0) -> dict:
    splits = jax.random.split(jax.random.key(seed), 13)
    return {
        "eta_pairs": noise(splits[0], (PAIRS, PAIRS), 1.0, 6.0, ((0, 4), (1, 8))),
        "gamma_pairs": noise(splits[1], (PAIRS, PAIRS), PAIRS ** -0.5, 0.0546875, ((0, 4), (1, 8))),
        "pair_first": with_ends(jax.random.randint(splits[2], (PAIRS,), 0, ORBITS), jax.random.fold_in(splits[2], 1), 0, ORBITS - 1).astype(jnp.int32),
        "pair_second": with_ends(jax.random.randint(splits[3], (PAIRS,), 0, ORBITS), jax.random.fold_in(splits[3], 1), 0, ORBITS - 1).astype(jnp.int32),
        "occupancy": jnp.clip(jax.random.uniform(splits[4], (ORBITS,), jnp.float32, 0.0, 1.0), 0.0, 1.0),
        "gamma_recoupled": noise(splits[5], (BLOCKS, PH_STATES, PH_STATES), PH_STATES ** -0.5, 0.15625, ((0, 32),)),
        "ph_factor": jnp.clip(jax.random.uniform(splits[6], (BLOCKS, PH_STATES), jnp.float32, -1.0, 1.0) * levels(splits[6], (BLOCKS, PH_STATES), ((0, 32),), -0.4, 0.0), -1.0, 1.0),
        "tile_source": draw_tile_source(jax.random.fold_in(splits[12], 71), 0),
        "tile_owner": draw_tile_owner(jax.random.fold_in(splits[12], 71), 0),
        "tile_place": with_ends(jax.random.randint(splits[9], (BLOCKS, SLOTS), 0, PH_TILES * PH_TILES), jax.random.fold_in(splits[9], 1), 0, (PH_TILES * PH_TILES) - 1).astype(jnp.int32),
        "sixj_weight": jnp.clip(jax.random.uniform(splits[10], (BLOCKS, SLOTS), jnp.float32, -1.0, 1.0) * levels(splits[10], (BLOCKS, SLOTS), ((0, 32),), -0.4, 0.0), -1.0, 1.0).astype(jnp.bfloat16),
        "live_count": draw_live_count(jax.random.fold_in(splits[12], 71), 0),
    }


def orbit_lookup(pair_ids, occupancy):
    orbit_ids = jnp.arange(ORBITS, dtype=jnp.int32)
    return jnp.sum(jnp.where(pair_ids[:, None] == orbit_ids[None, :], occupancy[None, :], 0.0), axis=1)


def reference(eta_pairs, gamma_pairs, pair_first, pair_second, occupancy, gamma_recoupled, ph_factor, tile_source, tile_owner, tile_place, sixj_weight, live_count):
    factor = 1.0 - orbit_lookup(pair_first, occupancy) - orbit_lookup(pair_second, occupancy)
    panel_ids = jnp.arange(PANEL, dtype=jnp.int32)
    columns = (panel_ids // PANEL_DEV) * BLOCK_COLS + panel_ids % PANEL_DEV
    gamma_panel = (factor[:, None] * gamma_pairs[:, columns].astype(jnp.float32)).astype(jnp.bfloat16)
    eta_panel = (factor[:, None] * eta_pairs[:, columns].astype(jnp.float32)).astype(jnp.bfloat16)
    panel_total = jnp.zeros((PANEL, PAIRS), jnp.float32)
    for column_block in range(N_COL):
        lower = column_block * BLOCK_COLS
        upper = lower + BLOCK_COLS
        block_sum = jnp.dot(eta_pairs[:, lower:upper], gamma_panel[lower:upper], preferred_element_type=jnp.float32)
        block_sum = block_sum - jnp.dot(gamma_pairs[:, lower:upper], eta_panel[lower:upper], preferred_element_type=jnp.float32)
        rounded = lax.optimization_barrier(block_sum.astype(jnp.bfloat16))
        panel_total = panel_total + rounded.T.astype(jnp.float32)
    panel_update = panel_total.astype(jnp.bfloat16)

    row_tiles = BLOCK_ROWS // TILE
    col_tiles = BLOCK_COLS // TILE
    eta_tiles = eta_pairs.reshape(N_ROW, row_tiles, TILE, N_COL, col_tiles, TILE)
    eta_tiles = eta_tiles.transpose(0, 3, 1, 4, 2, 5).reshape(BLOCKS, TILES_BLOCK, TILE, TILE)
    slot_ids = jnp.arange(SLOTS, dtype=jnp.int32)

    def add_block(accumulated, inputs):
        block_tiles, sources, owners, places, weights, live = inputs
        picked = block_tiles[sources]
        sent = (weights.astype(jnp.float32)[:, None, None] * picked.astype(jnp.float32)).astype(jnp.bfloat16)
        sent = lax.optimization_barrier(sent)
        is_live = slot_ids < live
        contrib = jnp.where(is_live[:, None, None], sent.astype(jnp.float32), 0.0)
        return accumulated.at[owners, places].add(contrib), None

    start_sums = jnp.zeros((BLOCKS, PH_TILES * PH_TILES, TILE, TILE), jnp.float32)
    accumulated, _ = lax.scan(add_block, start_sums, (eta_tiles, tile_source, tile_owner, tile_place, sixj_weight, live_count))
    eta_recoupled = accumulated.reshape(BLOCKS, PH_TILES, PH_TILES, TILE, TILE).transpose(0, 1, 3, 2, 4)
    eta_recoupled = eta_recoupled.reshape(BLOCKS, PH_STATES, PH_STATES).astype(jnp.bfloat16)

    def one_channel(inputs):
        eta_ph, gamma_ph, scale = inputs
        gamma_scaled = (scale[:, None] * gamma_ph.astype(jnp.float32)).astype(jnp.bfloat16)
        eta_scaled = (scale[:, None] * eta_ph.astype(jnp.float32)).astype(jnp.bfloat16)
        product = jnp.dot(eta_ph, gamma_scaled, preferred_element_type=jnp.float32)
        product = product - jnp.dot(gamma_ph, eta_scaled, preferred_element_type=jnp.float32)
        return product.astype(jnp.bfloat16)

    ph_product = lax.map(one_channel, (eta_recoupled, gamma_recoupled, ph_factor))
    product_tiles = ph_product.reshape(BLOCKS, PH_TILES, TILE, PH_TILES, TILE).transpose(0, 1, 3, 2, 4)
    product_tiles = product_tiles.reshape(BLOCKS, PH_TILES * PH_TILES, TILE, TILE)

    def back_block(inputs):
        sources, owners, places, weights, live = inputs
        picked = product_tiles[owners, places]
        is_live = slot_ids < live
        contrib = jnp.where(is_live[:, None, None], weights.astype(jnp.float32)[:, None, None] * picked.astype(jnp.float32), 0.0)
        gathered = jnp.zeros((TILES_BLOCK, TILE, TILE), jnp.float32).at[sources].add(contrib)
        return gathered.astype(jnp.bfloat16)

    updates = lax.map(back_block, (tile_source, tile_owner, tile_place, sixj_weight, live_count))
    updates = updates.reshape(N_ROW, N_COL, row_tiles, col_tiles, TILE, TILE).transpose(0, 2, 4, 1, 3, 5)
    recoupled_update = updates.reshape(PAIRS, PAIRS)
    return panel_update, recoupled_update
```

```python
import functools

import jax
import jax.numpy as jnp
from jax import lax
from jax.experimental import pallas as pl
from jax.experimental.pallas import tpu as pltpu
from jax.sharding import PartitionSpec as P

TILE = 128
PH_STATES = 1536
PANEL_DEV = 128
VMEM_BYTES = 56 * 1024 * 1024


def orbit_lookup(pair_ids, occupancy):
    orbit_ids = jnp.arange(occupancy.shape[0], dtype=jnp.int32)
    return jnp.sum(
        jnp.where(pair_ids[:, None] == orbit_ids[None, :], occupancy[None, :], 0.0), axis=1
    )


def panel_part(eta_pairs, gamma_pairs, pair_first, pair_second, occupancy):
    n_row = lax.axis_size("row")
    n_col = lax.axis_size("col")
    factor = 1.0 - orbit_lookup(pair_first, occupancy) - orbit_lookup(pair_second, occupancy)
    columns = jnp.concatenate([gamma_pairs[:, :PANEL_DEV], eta_pairs[:, :PANEL_DEV]], axis=1)
    columns = (factor[:, None] * columns.astype(jnp.float32)).astype(jnp.bfloat16).T
    columns = columns.reshape(2, PANEL_DEV, eta_pairs.shape[0])
    shares = lax.all_to_all(columns, "col", split_axis=2, concat_axis=1, tiled=True)
    ratio = n_col // n_row
    moves = [
        (i * n_col + j, (j % n_row) * n_col + i * ratio + j // n_row)
        for i in range(n_row)
        for j in range(n_col)
    ]
    shares = lax.ppermute(shares, ("row", "col"), moves)
    panels = lax.all_gather(shares, "row", axis=2, tiled=True)
    contract = (((1,), (1,)), ((), ()))
    leading = lax.dot_general(panels[0], eta_pairs, contract, preferred_element_type=jnp.float32)
    trailing = lax.dot_general(panels[1], gamma_pairs, contract, preferred_element_type=jnp.float32)
    return lax.psum_scatter(
        (leading - trailing).astype(jnp.bfloat16), "col", scatter_dimension=0, tiled=True
    )


def gather_kernel(capacity, col_tiles, ids_ref, weights_ref, matrix_ref, out_ref):
    first = pl.program_id(0) * capacity

    def one(k, carry):
        tile = jnp.maximum(ids_ref[first + k], 0)
        rows = pl.ds(pl.multiple_of((tile // col_tiles) * TILE, TILE), TILE)
        cols = pl.ds(pl.multiple_of((tile % col_tiles) * TILE, TILE), TILE)
        scaled = weights_ref[first + k] * matrix_ref[rows, cols].astype(jnp.float32)
        out_ref[0, k] = scaled.astype(jnp.bfloat16)
        return carry

    lax.fori_loop(0, capacity, one, 0, unroll=True)


def gather_tiles(matrix, ids, weights, blocks, capacity):
    smem = pl.BlockSpec(memory_space=pltpu.SMEM)
    return pl.pallas_call(
        functools.partial(gather_kernel, capacity, matrix.shape[1] // TILE),
        grid=(blocks,),
        in_specs=[smem, smem, pl.BlockSpec(matrix.shape, lambda g: (0, 0))],
        out_specs=pl.BlockSpec((1, capacity, TILE, TILE), lambda g: (g, 0, 0, 0)),
        out_shape=jax.ShapeDtypeStruct((blocks, capacity, TILE, TILE), jnp.bfloat16),
        compiler_params=pltpu.CompilerParams(vmem_limit_bytes=VMEM_BYTES),
        cost_estimate=pl.CostEstimate(
            flops=blocks * capacity * TILE * TILE,
            bytes_accessed=2 * (matrix.size + blocks * capacity * TILE * TILE),
            transcendentals=0,
        ),
        name="gather_tiles",
    )(ids, weights, matrix)


def scatter_kernel(capacity, col_tiles, ids_ref, weights_ref, tiles_ref, out_ref, total):
    step = pl.program_id(0)
    first = step * capacity

    @pl.when(step == 0)
    def _():
        total[...] = jnp.zeros_like(total)

    def one(k, carry):
        tile = ids_ref[first + k]

        @pl.when(tile >= 0)
        def _():
            rows = pl.ds(pl.multiple_of((tile // col_tiles) * TILE, TILE), TILE)
            cols = pl.ds(pl.multiple_of((tile % col_tiles) * TILE, TILE), TILE)
            total[rows, cols] += weights_ref[first + k] * tiles_ref[0, k].astype(jnp.float32)

        return carry

    lax.fori_loop(0, capacity, one, 0)

    @pl.when(step == pl.num_programs(0) - 1)
    def _():
        out_ref[...] = total[...].astype(jnp.bfloat16)


def scatter_tiles(tiles, ids, weights, shape):
    blocks, capacity = tiles.shape[:2]
    smem = pl.BlockSpec(memory_space=pltpu.SMEM)
    return pl.pallas_call(
        functools.partial(scatter_kernel, capacity, shape[1] // TILE),
        grid=(blocks,),
        in_specs=[
            smem,
            smem,
            pl.BlockSpec((1, capacity, TILE, TILE), lambda g: (g, 0, 0, 0)),
        ],
        out_specs=pl.BlockSpec(shape, lambda g: (0, 0)),
        out_shape=jax.ShapeDtypeStruct(shape, jnp.bfloat16),
        scratch_shapes=[pltpu.VMEM(shape, jnp.float32)],
        compiler_params=pltpu.CompilerParams(vmem_limit_bytes=VMEM_BYTES),
        cost_estimate=pl.CostEstimate(
            flops=2 * tiles.size,
            bytes_accessed=2 * (tiles.size + shape[0] * shape[1]),
            transcendentals=0,
        ),
        name="scatter_tiles",
    )(ids, weights, tiles)


def exchange(tiles):
    return lax.all_to_all(tiles, ("row", "col"), split_axis=0, concat_axis=0, tiled=True)


def recoupled_part(
    eta_pairs,
    gamma_recoupled,
    ph_factor,
    tile_source,
    tile_owner,
    tile_place,
    sixj_weight,
    live_count,
):
    blocks = lax.axis_size("row") * lax.axis_size("col")
    slot_total = tile_source.shape[1]
    capacity = max(2, (slot_total + blocks - 1) // blocks)
    sources = tile_source[0]
    owners = tile_owner[0]
    places = tile_place[0]
    weights = sixj_weight[0].astype(jnp.float32)
    slot_ids = jnp.arange(slot_total, dtype=jnp.int32)
    is_live = slot_ids < live_count[0]
    same_owner = (
        (owners[:, None] == owners[None, :])
        & is_live[None, :]
        & (slot_ids[None, :] < slot_ids[:, None])
    )
    slot_rank = jnp.sum(same_owner.astype(jnp.int32), axis=1)
    buffer_ids = jnp.arange(blocks * capacity, dtype=jnp.int32)
    slot_buffer = jnp.where(is_live, owners * capacity + slot_rank, -1)
    hit = buffer_ids[:, None] == slot_buffer[None, :]
    buffer_source = jnp.sum(jnp.where(hit, sources[None, :] + 1, 0), axis=1) - 1
    buffer_place = jnp.sum(jnp.where(hit, places[None, :] + 1, 0), axis=1) - 1
    buffer_weight = jnp.sum(jnp.where(hit, weights[None, :], 0.0), axis=1)
    codes = exchange(buffer_place.reshape(blocks, capacity)).reshape(blocks * capacity)
    ones = jnp.ones((blocks * capacity,), jnp.float32)
    sent = gather_tiles(eta_pairs, buffer_source, buffer_weight, blocks, capacity)
    eta_ph = scatter_tiles(exchange(sent), codes, ones, (PH_STATES, PH_STATES))
    gamma_ph = gamma_recoupled[0]
    scale = ph_factor[0]
    gamma_scaled = (scale[:, None] * gamma_ph.astype(jnp.float32)).astype(jnp.bfloat16)
    eta_scaled = (scale[:, None] * eta_ph.astype(jnp.float32)).astype(jnp.bfloat16)
    product = jnp.dot(eta_ph, gamma_scaled, preferred_element_type=jnp.float32)
    product = (product - jnp.dot(gamma_ph, eta_scaled, preferred_element_type=jnp.float32)).astype(
        jnp.bfloat16
    )
    answer = gather_tiles(product, codes, ones, blocks, capacity)
    return scatter_tiles(exchange(answer), buffer_source, buffer_weight, eta_pairs.shape)


def local(
    eta_pairs,
    gamma_pairs,
    pair_first,
    pair_second,
    occupancy,
    gamma_recoupled,
    ph_factor,
    tile_source,
    tile_owner,
    tile_place,
    sixj_weight,
    live_count,
):
    panel_update = panel_part(eta_pairs, gamma_pairs, pair_first, pair_second, occupancy)
    recoupled_update = recoupled_part(
        eta_pairs,
        gamma_recoupled,
        ph_factor,
        tile_source,
        tile_owner,
        tile_place,
        sixj_weight,
        live_count,
    )
    return (panel_update, recoupled_update)


def solution(mesh):
    in_specs = (
        P("row", "col"),
        P("row", "col"),
        P("row"),
        P("row"),
        P(),
        P(("row", "col"), None, None),
        P(("row", "col"), None),
        P(("row", "col"), None),
        P(("row", "col"), None),
        P(("row", "col"), None),
        P(("row", "col"), None),
        P(("row", "col")),
    )
    out_specs = (P("col", "row"), P("row", "col"))
    return jax.shard_map(local, mesh=mesh, in_specs=in_specs, out_specs=out_specs, check_vma=False)
```

```python
import functools

import jax
import jax.numpy as jnp
from jax import lax
from jax.experimental import pallas as pl
from jax.experimental.pallas import tpu as pltpu
from jax.sharding import PartitionSpec as P

TILE = 128
PH_STATES = 1536
PANEL_DEV = 128
VMEM_BYTES = 56 * 1024 * 1024


def orbit_lookup(pair_ids, occupancy):
    orbit_ids = jnp.arange(occupancy.shape[0], dtype=jnp.int32)
    return jnp.sum(
        jnp.where(pair_ids[:, None] == orbit_ids[None, :], occupancy[None, :], 0.0), axis=1
    )


def panel_shares(eta_pairs, gamma_pairs, pair_first, pair_second, occupancy):
    factor = 1.0 - orbit_lookup(pair_first, occupancy) - orbit_lookup(pair_second, occupancy)
    columns = jnp.concatenate([gamma_pairs[:, :PANEL_DEV], eta_pairs[:, :PANEL_DEV]], axis=1)
    columns = (factor[:, None] * columns.astype(jnp.float32)).astype(jnp.bfloat16).T
    columns = columns.reshape(2, PANEL_DEV, eta_pairs.shape[0])
    return lax.all_to_all(columns, "col", split_axis=2, concat_axis=1, tiled=True)


def panel_gather(shares):
    n_row = lax.axis_size("row")
    n_col = lax.axis_size("col")
    ratio = n_col // n_row
    moves = [
        (i * n_col + j, (j % n_row) * n_col + i * ratio + j // n_row)
        for i in range(n_row)
        for j in range(n_col)
    ]
    shares = lax.ppermute(shares, ("row", "col"), moves)
    return lax.all_gather(shares, "row", axis=2, tiled=True)


def panel_product(panels, eta_pairs, gamma_pairs):
    contract = (((1,), (1,)), ((), ()))
    leading = lax.dot_general(panels[0], eta_pairs, contract, preferred_element_type=jnp.float32)
    trailing = lax.dot_general(panels[1], gamma_pairs, contract, preferred_element_type=jnp.float32)
    return lax.psum_scatter(
        (leading - trailing).astype(jnp.bfloat16), "col", scatter_dimension=0, tiled=True
    )


def gather_kernel(capacity, col_tiles, ids_ref, weights_ref, matrix_ref, out_ref):
    first = pl.program_id(0) * capacity

    def one(k, carry):
        tile = jnp.maximum(ids_ref[first + k], 0)
        rows = pl.ds(pl.multiple_of((tile // col_tiles) * TILE, TILE), TILE)
        cols = pl.ds(pl.multiple_of((tile % col_tiles) * TILE, TILE), TILE)
        scaled = weights_ref[first + k] * matrix_ref[rows, cols].astype(jnp.float32)
        out_ref[0, k] = scaled.astype(jnp.bfloat16)
        return carry

    lax.fori_loop(0, capacity, one, 0, unroll=True)


def gather_tiles(matrix, ids, weights, blocks, capacity):
    smem = pl.BlockSpec(memory_space=pltpu.SMEM)
    return pl.pallas_call(
        functools.partial(gather_kernel, capacity, matrix.shape[1] // TILE),
        grid=(blocks,),
        in_specs=[smem, smem, pl.BlockSpec(matrix.shape, lambda g: (0, 0))],
        out_specs=pl.BlockSpec((1, capacity, TILE, TILE), lambda g: (g, 0, 0, 0)),
        out_shape=jax.ShapeDtypeStruct((blocks, capacity, TILE, TILE), jnp.bfloat16),
        compiler_params=pltpu.CompilerParams(vmem_limit_bytes=VMEM_BYTES),
        cost_estimate=pl.CostEstimate(
            flops=blocks * capacity * TILE * TILE,
            bytes_accessed=2 * (matrix.size + blocks * capacity * TILE * TILE),
            transcendentals=0,
        ),
        name="gather_tiles",
    )(ids, weights, matrix)


def scatter_kernel(capacity, col_tiles, ids_ref, weights_ref, *refs):
    tiles_refs, out_ref, total = refs[:-2], refs[-2], refs[-1]
    step = pl.program_id(0)
    first = step * capacity
    part_steps = pl.num_programs(0) // len(tiles_refs)

    @pl.when(step == 0)
    def _():
        total[...] = jnp.zeros_like(total)

    def add_block(tiles_ref):
        def one(k, carry):
            tile = ids_ref[first + k]

            @pl.when(tile >= 0)
            def _():
                rows = pl.ds(pl.multiple_of((tile // col_tiles) * TILE, TILE), TILE)
                cols = pl.ds(pl.multiple_of((tile % col_tiles) * TILE, TILE), TILE)
                total[rows, cols] += weights_ref[first + k] * tiles_ref[0, k].astype(jnp.float32)

            return carry

        lax.fori_loop(0, capacity, one, 0)

    for part, tiles_ref in enumerate(tiles_refs):
        pl.when(step // part_steps == part)(functools.partial(add_block, tiles_ref))

    @pl.when(step == pl.num_programs(0) - 1)
    def _():
        out_ref[...] = total[...].astype(jnp.bfloat16)


def part_spec(part, blocks, capacity):
    return pl.BlockSpec(
        (1, capacity, TILE, TILE),
        lambda g: (jnp.clip(g - part * blocks, 0, blocks - 1), 0, 0, 0),
    )


def scatter_tiles(parts, ids, weights, shape):
    blocks, capacity = parts[0].shape[:2]
    smem = pl.BlockSpec(memory_space=pltpu.SMEM)
    size = len(parts) * parts[0].size
    return pl.pallas_call(
        functools.partial(scatter_kernel, capacity, shape[1] // TILE),
        grid=(len(parts) * blocks,),
        in_specs=[smem, smem] + [part_spec(p, blocks, capacity) for p in range(len(parts))],
        out_specs=pl.BlockSpec(shape, lambda g: (0, 0)),
        out_shape=jax.ShapeDtypeStruct(shape, jnp.bfloat16),
        scratch_shapes=[pltpu.VMEM(shape, jnp.float32)],
        compiler_params=pltpu.CompilerParams(vmem_limit_bytes=VMEM_BYTES),
        cost_estimate=pl.CostEstimate(
            flops=2 * size,
            bytes_accessed=2 * (size + shape[0] * shape[1]),
            transcendentals=0,
        ),
        name="scatter_tiles",
    )(ids, weights, *parts)


def half_groups():
    n_row = lax.axis_size("row")
    n_col = lax.axis_size("col")
    half = n_col // 2
    return [
        [i * n_col + h * half + j for i in range(n_row) for j in range(half)] for h in range(2)
    ]


def exchange(tiles, axis=0):
    return lax.all_to_all(
        tiles,
        ("row", "col"),
        split_axis=axis,
        concat_axis=axis,
        axis_index_groups=half_groups(),
        tiled=True,
    )


def mirror(matrix):
    n_col = lax.axis_size("col")
    return lax.ppermute(matrix, "col", [(j, (j + n_col // 2) % n_col) for j in range(n_col)])


def recoupled_part(
    shares,
    eta_pairs,
    gamma_recoupled,
    ph_factor,
    tile_source,
    tile_owner,
    tile_place,
    sixj_weight,
    live_count,
):
    n_col = lax.axis_size("col")
    blocks = lax.axis_size("row") * n_col
    near = blocks // 2
    half = n_col // 2
    slot_total = tile_source.shape[1]
    capacity = max(2, (slot_total + blocks - 1) // blocks)
    sources = tile_source[0]
    owners = tile_owner[0]
    places = tile_place[0]
    weights = sixj_weight[0].astype(jnp.float32)
    slot_ids = jnp.arange(slot_total, dtype=jnp.int32)
    is_live = slot_ids < live_count[0]
    same_owner = (
        (owners[:, None] == owners[None, :])
        & is_live[None, :]
        & (slot_ids[None, :] < slot_ids[:, None])
    )
    slot_rank = jnp.sum(same_owner.astype(jnp.int32), axis=1)
    buffer_ids = jnp.arange(blocks * capacity, dtype=jnp.int32)
    owner_col = owners % n_col
    is_far = (owner_col // half != lax.axis_index("col") // half).astype(jnp.int32)
    owner_at = is_far * near + (owners // n_col) * half + owner_col % half
    slot_buffer = jnp.where(is_live, owner_at * capacity + slot_rank, -1)
    hit = buffer_ids[:, None] == slot_buffer[None, :]
    buffer_source = jnp.sum(jnp.where(hit, sources[None, :] + 1, 0), axis=1) - 1
    buffer_place = jnp.sum(jnp.where(hit, places[None, :] + 1, 0), axis=1) - 1
    buffer_weight = jnp.sum(jnp.where(hit, weights[None, :], 0.0), axis=1)
    codes = exchange(buffer_place.reshape(2, near, capacity), 1).reshape(2, near * capacity)
    near_codes, far_codes = codes[0], codes[1]
    split = near * capacity
    ones = jnp.ones((split,), jnp.float32)
    ph_shape = (PH_STATES, PH_STATES)
    far_sent = gather_tiles(
        eta_pairs, buffer_source[split:], buffer_weight[split:], near, capacity
    )
    far_sum = scatter_tiles([exchange(far_sent)], far_codes, ones, ph_shape)
    near_weight, shares, far_sum = lax.optimization_barrier(
        (buffer_weight[:split], shares, far_sum)
    )
    moved = mirror(far_sum)
    near_sent = gather_tiles(eta_pairs, buffer_source[:split], near_weight, near, capacity)
    near_sum = scatter_tiles([exchange(near_sent)], near_codes, ones, ph_shape)
    panels = panel_gather(shares)
    moved, panels = lax.optimization_barrier((moved, panels))
    eta_ph = (near_sum.astype(jnp.float32) + moved.astype(jnp.float32)).astype(jnp.bfloat16)
    gamma_ph = gamma_recoupled[0]
    scale = ph_factor[0]
    gamma_scaled = (scale[:, None] * gamma_ph.astype(jnp.float32)).astype(jnp.bfloat16)
    eta_scaled = (scale[:, None] * eta_ph.astype(jnp.float32)).astype(jnp.bfloat16)
    product = jnp.dot(eta_ph, gamma_scaled, preferred_element_type=jnp.float32)
    product = (product - jnp.dot(gamma_ph, eta_scaled, preferred_element_type=jnp.float32)).astype(
        jnp.bfloat16
    )
    moved_product = mirror(product)
    near_back = exchange(gather_tiles(product, near_codes, ones, near, capacity))
    far_back = exchange(gather_tiles(moved_product, far_codes, ones, near, capacity))
    update = scatter_tiles(
        [near_back, far_back], buffer_source, buffer_weight, eta_pairs.shape
    )
    return panels, update


def local(
    eta_pairs,
    gamma_pairs,
    pair_first,
    pair_second,
    occupancy,
    gamma_recoupled,
    ph_factor,
    tile_source,
    tile_owner,
    tile_place,
    sixj_weight,
    live_count,
):
    shares = panel_shares(eta_pairs, gamma_pairs, pair_first, pair_second, occupancy)
    panels, recoupled_update = recoupled_part(
        shares,
        eta_pairs,
        gamma_recoupled,
        ph_factor,
        tile_source,
        tile_owner,
        tile_place,
        sixj_weight,
        live_count,
    )
    panel_update = panel_product(panels, eta_pairs, gamma_pairs)
    return (panel_update, recoupled_update)


def solution(mesh):
    in_specs = (
        P("row", "col"),
        P("row", "col"),
        P("row"),
        P("row"),
        P(),
        P(("row", "col"), None, None),
        P(("row", "col"), None),
        P(("row", "col"), None),
        P(("row", "col"), None),
        P(("row", "col"), None),
        P(("row", "col"), None),
        P(("row", "col")),
    )
    out_specs = (P("col", "row"), P("row", "col"))
    return jax.shard_map(local, mesh=mesh, in_specs=in_specs, out_specs=out_specs, check_vma=False)
```
